512 devices in a mesh: replica: 32 (over z_hi, x, core), fsdp: 16 (over y, z_lo).
Axes of the slice: x: 4, y: 8, z: 8 (z_hi: 4, z_lo: 2; z = z_hi * 2 + z_lo), core: 2. Of those that a mesh axis runs over, the one named last changes fastest.
Arguments:
- tokens: bfloat16 [65536, 4096], P(('replica', 'fsdp')), may hold values from -6 to 6
- cotangent: bfloat16 [65536, 512], P(('replica', 'fsdp')), may hold values from -6 to 6
- weight: float32 [32, 4096, 512], P('replica', 'fsdp'), may hold values from -3 to 3
- moment: bfloat16 [32, 4096, 512], P('replica', 'fsdp'), may hold values from -1.5 to 1.5
- second: bfloat16 [32, 4096, 512], P('replica', 'fsdp'), may hold values from 0.25 to 1
- outer_params: bfloat16 [4096, 512], P('fsdp'), may hold values from -6 to 6
- momentum: bfloat16 [4096, 512], P('fsdp'), may hold values from -3 to 3
Outputs:
- projected: bfloat16 [65536, 512], P(('replica', 'fsdp'))
- input_grad: bfloat16 [65536, 4096], P(('replica', 'fsdp'))
- new_weight: float32 [32, 4096, 512], P('replica', 'fsdp')
- new_moment: bfloat16 [32, 4096, 512], P('replica', 'fsdp')
- new_second: bfloat16 [32, 4096, 512], P('replica', 'fsdp')
The draws below stay inside these ranges and needn't reach their ends.
All inputs are finite; a program needn't handle non-finite values.
Results may differ from the reference program's by a relative error of at most 0.0049.
Values may be sent and summed in bfloat16 or wider, within the bound.
No kernel may reach another device: no remote copies, remote signals or barrier semaphores. Data moves between devices by JAX's collectives and lax.ppermute only.
A program may use at most 64 MiB of HBM per device.

```python
import math
import jax
import jax.numpy as jnp
from jax import lax

D = 4096
KV = 512
REPLICAS = 32
TOKENS = 65536
N_REPLICA = 32


def shard_levels(key, dims, cuts, least, top_value):
    def one(axis_at, parts):
        draws = jax.random.uniform(jax.random.fold_in(jax.random.fold_in(key, 6), axis_at), (parts,), jnp.float32, least / len(cuts), top_value / len(cuts))
        return jnp.repeat(jnp.exp(draws), dims[axis_at] // parts).reshape((-1,) + (1,) * (len(dims) - axis_at - 1))

    level = one(*cuts[0])
    for cut in cuts[1:]:
        level = level * one(*cut)
    return level


def noise(key, dims, spread, most, cuts=(), dtype=jnp.bfloat16):
    entries = jax.random.normal(key, dims, jnp.float32) * spread
    if len(cuts) > 0:
        entries = shard_levels(key, dims, cuts, -0.22, 0.18) * entries
    return jnp.clip(entries, min=-most, max=most).astype(dtype)


def setup_inputs(seed: int = 0) -> dict:
    key_list = jax.random.split(jax.random.key(seed), 8)
    return {
        "tokens": noise(key_list[0], (TOKENS, D), 1.0, 6.0, ((0, 512),)),
        "cotangent": noise(key_list[1], (TOKENS, KV), 1.0, 6.0, ((0, 512),)),
        "weight": noise(key_list[2], (REPLICAS, D, KV), 0.5, 3.0, ((0, 32), (1, 16)), jnp.float32),
        "moment": noise(key_list[3], (REPLICAS, D, KV), 0.25, 1.5, ((0, 32), (1, 16))),
        "second": jnp.clip(jnp.exp(math.log(1.0) - 1.3862944 * jax.random.uniform(key_list[4], (REPLICAS, D, KV), jnp.float32) ** shard_levels(key_list[4], (REPLICAS, D, KV), ((0, 32), (1, 16)), -0.2, 0.2)), 0.25, 1.0).astype(jnp.bfloat16),
        "outer_params": noise(key_list[5], (D, KV), 1.0, 6.0, ((0, 16),)),
        "momentum": noise(key_list[6], (D, KV), 0.5, 3.0, ((0, 16),)),
    }


def reference(tokens, cotangent, weight, moment, second, outer_params, momentum):
    factor = 1.0 / math.sqrt(D)
    token_blocks = tokens.reshape(N_REPLICA, -1, D)
    grad_blocks = cotangent.reshape(N_REPLICA, -1, KV)
    outer_wide = outer_params.astype(jnp.float32)
    average = lax.optimization_barrier(jnp.sum(outer_wide[None] - weight, axis=0)) / N_REPLICA
    velocity = 0.9 * momentum.astype(jnp.float32) + average
    outer_new = outer_wide - 0.7 * (average + 0.9 * velocity)

    def one_replica(items):
        token_rows, grad_rows, params, first, squares = items
        compute_weight = params.astype(jnp.bfloat16)
        projected = (jnp.dot(token_rows, compute_weight, preferred_element_type=jnp.float32) * factor).astype(jnp.bfloat16)
        input_grad = (jnp.dot(grad_rows, compute_weight.T, preferred_element_type=jnp.float32) * factor).astype(jnp.bfloat16)
        grad = jnp.dot(token_rows.T, grad_rows, preferred_element_type=jnp.float32) * factor
        first_new = 0.8 * first.astype(jnp.float32) + 0.2 * grad
        second_new = 0.95 * squares.astype(jnp.float32) + 0.05 * grad * grad
        inner = params - 0.05 * (first_new / (jnp.sqrt(second_new) + 1e-08) + 0.1 * params)
        merged = 0.5 * inner + 0.5 * outer_new
        return (projected, input_grad, merged, first_new.astype(jnp.bfloat16), second_new.astype(jnp.bfloat16))
    projected, input_grad, new_weight, new_moment, new_second = lax.map(one_replica, (token_blocks, grad_blocks, weight, moment, second))
    return (projected.reshape(-1, KV), input_grad.reshape(-1, D), new_weight, new_moment, new_second)
```

```python
import math

import jax
import jax.numpy as jnp
from jax import lax
from jax.sharding import Mesh, PartitionSpec as P

SIZES = (4, 4, 2, 8, 2)
NAMES = ("zh", "x", "core", "y", "zl")
REPLICA = ("zh", "x", "core")
FSDP = ("y", "zl")
PAIR = [(0, 1), (1, 0)]
BF16 = jnp.bfloat16
F32 = jnp.float32


def replica_mean(rows):
    replicas = lax.axis_size(REPLICA)
    parts = rows.reshape(replicas, -1, rows.shape[-1])
    mine = lax.all_to_all(parts, REPLICA, 0, 0, tiled=True)
    mean = (jnp.sum(mine.astype(F32), axis=0) / replicas).astype(BF16)
    out = lax.all_to_all(jnp.broadcast_to(mean[None], parts.shape), REPLICA, 0, 0, tiled=True)
    return out.reshape(rows.shape).astype(F32)


def body(tokens, cotangent, weight, moment, second, outer_params, momentum):
    n_tok, model_width = tokens.shape
    kv = cotangent.shape[1]
    factor = 1.0 / math.sqrt(model_width)
    ys = lax.axis_size("y")
    zl = lax.axis_index("zl")
    local_rows = weight[0]
    rows = local_rows.shape[0]
    half = ys * rows
    compute_rows = local_rows.astype(BF16)

    both = lax.all_gather(jnp.concatenate([compute_rows, cotangent], 0), "y", axis=0, tiled=False)
    w_half = both[:, :rows].reshape(half, kv)
    cot_y = both[:, rows:].reshape(ys * n_tok, kv)

    blocks = tokens.reshape(n_tok, ys, 2, rows)
    own = jnp.where(zl == 0, blocks[:, :, 0], blocks[:, :, 1]).reshape(n_tok, half)
    other = jnp.where(zl == 0, blocks[:, :, 1], blocks[:, :, 0]).reshape(n_tok, half)
    got = lax.ppermute(jnp.concatenate([other, cotangent], 1), "zl", PAIR)

    slab = lax.all_to_all(tokens, "y", split_axis=1, concat_axis=0, tiled=True)
    mean_rows = replica_mean(compute_rows)

    forward = jnp.dot(got[:, :half], w_half, preferred_element_type=F32)
    back = lax.dot_general(got[:, half:], w_half, (((1,), (1,)), ((), ())), preferred_element_type=F32)
    returned = lax.ppermute(
        jnp.concatenate([(back * factor).astype(BF16), (forward * factor).astype(BF16)], 1), "zl", PAIR
    )
    forward_own = jnp.dot(own, w_half, preferred_element_type=F32)
    back_own = lax.dot_general(cotangent, w_half, (((1,), (1,)), ((), ())), preferred_element_type=F32)

    partial = lax.dot_general(slab, cot_y, (((0,), (0,)), ((), ())), preferred_element_type=F32) * factor
    partial_own = jnp.where(zl == 0, partial[:rows], partial[rows:])
    partial_other = jnp.where(zl == 0, partial[rows:], partial[:rows]).astype(BF16)
    grad = partial_own + lax.ppermute(partial_other, "zl", PAIR).astype(F32)

    outer_wide = outer_params.astype(F32)
    average = outer_wide - mean_rows
    velocity = 0.9 * momentum.astype(F32) + average
    outer_new = outer_wide - 0.7 * (average + 0.9 * velocity)
    first_new = 0.8 * moment[0].astype(F32) + 0.2 * grad
    second_new = 0.95 * second[0].astype(F32) + 0.05 * grad * grad
    inner = local_rows - 0.05 * (first_new / (jnp.sqrt(second_new) + 1e-08) + 0.1 * local_rows)
    merged = 0.5 * inner + 0.5 * outer_new

    projected = (forward_own * factor + returned[:, half:].astype(F32)).astype(BF16)
    mine = (back_own * factor).astype(BF16).reshape(n_tok, ys, rows)
    theirs = returned[:, :half].reshape(n_tok, ys, rows)
    input_grad = jnp.where(
        zl == 0, jnp.stack([mine, theirs], 2), jnp.stack([theirs, mine], 2)
    ).reshape(n_tok, model_width)
    return (
        projected,
        input_grad,
        merged[None],
        first_new.astype(BF16)[None],
        second_new.astype(BF16)[None],
    )


def solution(mesh):
    fine = Mesh(mesh.devices.reshape(SIZES), NAMES)
    tok = P(NAMES, None)
    par = P(REPLICA, FSDP, None)
    outer = P(FSDP, None)
    return jax.shard_map(
        body,
        mesh=fine,
        in_specs=(tok, tok, par, par, par, outer, outer),
        out_specs=(tok, tok, par, par, par),
        check_vma=False,
    )
```

```python
import functools
import math

import jax
import jax.numpy as jnp
from jax import lax
from jax.experimental import pallas as pl
from jax.experimental.pallas import tpu as pltpu
from jax.sharding import Mesh, PartitionSpec as P

SIZES = (4, 4, 2, 8, 2)
NAMES = ("zh", "x", "core", "y", "zl")
REPLICA = ("zh", "x", "core")
FSDP = ("y", "zl")
PAIR = [(0, 1), (1, 0)]
BF16 = jnp.bfloat16
F32 = jnp.float32
YS = 8
ROWS = 256
TOK = 128
KV = 512
MIB = 1 << 20


def shift(k):
    return [(i, (i + k) % YS) for i in range(YS)]


def whole(shape):
    return pl.BlockSpec(shape, lambda i, s: (0,) * len(shape))


TOP = pl.BlockSpec((ROWS, KV), lambda i, s: (0, 0))
LOW = pl.BlockSpec((ROWS, KV), lambda i, s: (1, 0))


def call(kernel, place, args, in_specs, outs, flops, scratch=()):
    size = sum(math.prod(a.shape) * a.dtype.itemsize for a in args)
    size += sum(math.prod(o.shape) * o.dtype.itemsize for o in outs)
    return pl.pallas_call(
        kernel,
        out_shape=outs,
        grid_spec=pltpu.PrefetchScalarGridSpec(
            num_scalar_prefetch=1,
            grid=(1,),
            in_specs=in_specs,
            out_specs=[whole(o.shape) for o in outs],
            scratch_shapes=scratch,
        ),
        compiler_params=pltpu.CompilerParams(vmem_limit_bytes=40 * MIB),
        cost_estimate=pl.CostEstimate(flops=flops, bytes_accessed=size, transcendentals=0),
    )(place, *args)


def lanes(index):
    return pl.ds(pl.multiple_of(index * ROWS, ROWS), ROWS)


def split_kernel(place, tok, blocks, other):
    zl = place[1]
    for f in range(2 * YS):
        blocks[f] = tok[:, f * ROWS : (f + 1) * ROWS]
    for f in range(YS):
        other[:, f * ROWS : (f + 1) * ROWS] = tok[:, lanes(2 * f + 1 - zl)]


def block_products(place, k, factor, tok, got, cots, w):
    f = lax.rem(place[0] + k + YS, YS)
    x = jnp.concatenate([tok[:, lanes(2 * f + place[1])], got[:, lanes(f)]], 0)
    ahead = jnp.dot(x, w, preferred_element_type=F32)
    back = lax.dot_general(cots, w, (((1,), (1,)), ((), ())), preferred_element_type=F32)
    return ahead, (back * factor).astype(BF16)


def near_kernel(ks, factor, place, tok, got, cot, cot_got, *refs):
    w_refs, (back_own, back_got, ahead) = refs[: len(ks)], refs[len(ks) :]
    cots = jnp.concatenate([cot[...], cot_got[...]], 0)
    for i, k in enumerate(ks):
        a, b = block_products(place, k, factor, tok, got, cots, w_refs[i][...])
        back_own[:, i * ROWS : (i + 1) * ROWS] = b[:TOK]
        back_got[:, i * ROWS : (i + 1) * ROWS] = b[TOK:]
        ahead[...] = a if i == 0 else ahead[...] + a


def far_kernel(k, factor, place, tok, got, cot, cot_got, w, ahead, ahead_own, back_own, back):
    cots = jnp.concatenate([cot[...], cot_got[...]], 0)
    a, b = block_products(place, k, factor, tok, got, cots, w[...])
    total = (ahead[...] + a) * factor
    ahead_own[...] = total[:TOK]
    back_own[...] = b[:TOK]
    back[:, :ROWS] = b[TOK:]
    back[:, ROWS:] = total[TOK:].astype(BF16)


def join_kernel(ks, place, own_near, got_near, own_far, far, ahead_own, projected, input_grad):
    zl = place[1]
    for i, k in enumerate(ks):
        f = lax.rem(place[0] + k + YS, YS)
        near = i < len(ks) - 1
        cols = slice(i * ROWS, (i + 1) * ROWS)
        input_grad[:, lanes(2 * f + zl)] = own_near[:, cols] if near else own_far[...]
        input_grad[:, lanes(2 * f + 1 - zl)] = got_near[:, cols] if near else far[:, :ROWS]
    projected[...] = (ahead_own[...] + far[:, ROWS:].astype(F32)).astype(BF16)


def step_kernel(ks, factor, place, slab, weight, moment, second, outer, momentum, mean, *refs):
    c_refs, (new_weight, new_moment, new_second) = refs[: len(ks)], refs[len(ks) :]
    total = None
    for i, k in enumerate(ks):
        f = lax.rem(place[0] + k + YS, YS)
        x = slab[pl.ds(2 * f, 2)].reshape(2 * TOK, ROWS)
        part = lax.dot_general(x, c_refs[i][...], (((0,), (0,)), ((), ())), preferred_element_type=F32)
        total = part if i == 0 else total + part
    grad = total * factor
    local = weight[...]
    outer_wide = outer[...].astype(F32)
    average = outer_wide - mean[...].astype(F32)
    velocity = 0.9 * momentum[...].astype(F32) + average
    outer_new = outer_wide - 0.7 * (average + 0.9 * velocity)
    first_new = 0.8 * moment[...].astype(F32) + 0.2 * grad
    second_new = 0.95 * second[...].astype(F32) + 0.05 * grad * grad
    inner = local - 0.05 * (first_new / (jnp.sqrt(second_new) + 1e-08) + 0.1 * local)
    new_weight[...] = 0.5 * inner + 0.5 * outer_new
    new_moment[...] = first_new.astype(BF16)
    new_second[...] = second_new.astype(BF16)


def replica_mean(rows):
    replicas = lax.axis_size(REPLICA)
    parts = rows.reshape(replicas, -1, rows.shape[-1])
    mine = lax.all_to_all(parts, REPLICA, 0, 0, tiled=True)
    mean = (jnp.sum(mine.astype(F32), axis=0) / replicas).astype(BF16)
    out = lax.all_to_all(jnp.broadcast_to(mean[None], parts.shape), REPLICA, 0, 0, tiled=True)
    return out.reshape(rows.shape)


def body(tokens, cotangent, weight, moment, second, outer_params, momentum):
    factor = 1.0 / math.sqrt(tokens.shape[1])
    zl = lax.axis_index("zl")
    place = jnp.stack([lax.axis_index("y"), zl]).astype(jnp.int32)
    sds = jax.ShapeDtypeStruct
    compute_rows = weight[0].astype(BF16)

    cot_got = lax.ppermute(cotangent, "zl", PAIR)
    blocks, other = call(
        split_kernel, place, [tokens], [whole(tokens.shape)],
        [sds((2 * YS, TOK, ROWS), BF16), sds((TOK, YS * ROWS), BF16)], 0,
    )
    first = jnp.where(zl == 0, cotangent, cot_got)
    last = jnp.where(zl == 0, cot_got, cotangent)
    home = jnp.concatenate([compute_rows, first, last], 0)

    up, down = [home], [home]
    for _ in range(3):
        up.append(lax.ppermute(up[-1], "y", shift(1)))
        down.append(lax.ppermute(down[-1], "y", shift(-1)))
    far_w = lax.ppermute(up[3][:ROWS], "y", shift(1))
    far_c = lax.ppermute(down[3][ROWS:], "y", shift(-1))

    got = lax.ppermute(other, "zl", PAIR)
    blocks, _ = lax.optimization_barrier((blocks, up[1]))
    slab = lax.all_to_all(blocks, FSDP, 0, 0, tiled=True)
    mean_rows = replica_mean(compute_rows)

    ks = (0, -1, 1, -2, 2, -3, 3)
    near = [home, up[1], down[1], up[2], down[2], up[3], down[3]]
    flops = 4 * 2 * TOK * ROWS * KV
    common = [tokens, got, cotangent, cot_got]
    common_specs = [whole(a.shape) for a in common]
    back_own, back_got, ahead = call(
        functools.partial(near_kernel, ks, factor), place, common + near, common_specs + [TOP] * 7,
        [sds((TOK, 7 * ROWS), BF16), sds((TOK, 7 * ROWS), BF16), sds((2 * TOK, KV), F32)], 7 * flops,
    )
    near_back = lax.ppermute(back_got, "zl", PAIR)
    ahead_own, far_own, far_got = call(
        functools.partial(far_kernel, 4, factor), place, common + [far_w, ahead],
        common_specs + [whole(far_w.shape), whole(ahead.shape)],
        [sds((TOK, KV), F32), sds((TOK, ROWS), BF16), sds((TOK, ROWS + KV), BF16)], flops,
    )
    far_back = lax.ppermute(far_got, "zl", PAIR)

    states = [slab, weight[0], moment[0], second[0], outer_params, momentum, mean_rows]
    new_weight, new_moment, new_second = call(
        functools.partial(step_kernel, ks + (4,), factor), place, states + near + [far_c],
        [whole(a.shape) for a in states] + [LOW] * 7 + [whole(far_c.shape)],
        [sds((ROWS, KV), F32), sds((ROWS, KV), BF16), sds((ROWS, KV), BF16)], 8 * flops // 2,
    )
    parts = [back_own, near_back, far_own, far_back, ahead_own]
    projected, input_grad = call(
        functools.partial(join_kernel, ks + (4,)), place, parts, [whole(a.shape) for a in parts],
        [sds((TOK, KV), BF16), sds(tokens.shape, BF16)], 0,
    )
    return projected, input_grad, new_weight[None], new_moment[None], new_second[None]


def solution(mesh):
    fine = Mesh(mesh.devices.reshape(SIZES), NAMES)
    tok = P(NAMES, None)
    par = P(REPLICA, FSDP, None)
    outer = P(FSDP, None)
    return jax.shard_map(
        body,
        mesh=fine,
        in_specs=(tok, tok, par, par, par, outer, outer),
        out_specs=(tok, tok, par, par, par),
        check_vma=False,
    )
```

```python
import functools
import math

import jax
import jax.numpy as jnp
from jax import lax
from jax.experimental import pallas as pl
from jax.experimental.pallas import tpu as pltpu
from jax.sharding import Mesh, PartitionSpec as P

SIZES = (4, 4, 2, 8, 2)
NAMES = ("zh", "x", "core", "y", "zl")
REPLICA = ("zh", "x", "core")
FSDP = ("y", "zl")
PAIR = [(0, 1), (1, 0)]
BF16 = jnp.bfloat16
F32 = jnp.float32
YS = 8
REPLICAS = 32
ROWS = 256
TOK = 128
KV = 512
MIB = 1 << 20


def whole(shape):
    return pl.BlockSpec(shape, lambda *_: (0,) * len(shape))


def call(kernel, place, args, in_specs, outs, flops, scratch=()):
    size = sum(math.prod(a.shape) * a.dtype.itemsize for a in args)
    size += sum(math.prod(o.shape) * o.dtype.itemsize for o in outs)
    return pl.pallas_call(
        kernel,
        out_shape=outs,
        grid_spec=pltpu.PrefetchScalarGridSpec(
            num_scalar_prefetch=0 if place is None else 1,
            grid=(1,),
            in_specs=in_specs,
            out_specs=[whole(o.shape) for o in outs],
            scratch_shapes=scratch,
        ),
        compiler_params=pltpu.CompilerParams(vmem_limit_bytes=56 * MIB),
        cost_estimate=pl.CostEstimate(flops=flops, bytes_accessed=size, transcendentals=0),
    )(*([] if place is None else [place]), *args)


def lanes(index):
    return pl.ds(pl.multiple_of(index * ROWS, ROWS), ROWS)


def pack_kernel(weight, cot, packed):
    packed[:ROWS] = weight[...].astype(BF16)
    packed[ROWS:] = cot[...]


def split_kernel(place, tok, cot, blocks, other):
    other[:, YS * ROWS :] = cot[...]
    for f in range(YS):
        blocks[f] = tok[:, 2 * f * ROWS : (2 * f + 2) * ROWS]
        other[:, f * ROWS : (f + 1) * ROWS] = tok[:, lanes(2 * f + 1 - place[1])]


def product_kernel(factor, place, tok, cot, got, both, own, ahead, to_return):
    cots = jnp.concatenate([cot[...], got[:, YS * ROWS :]], 0)
    total = None
    for f in range(YS):
        w = both[f, :ROWS]
        cols = slice(f * ROWS, (f + 1) * ROWS)
        x = jnp.concatenate([tok[:, lanes(2 * f + place[1])], got[:, cols]], 0)
        part = jnp.dot(x, w, preferred_element_type=F32)
        total = part if f == 0 else total + part
        ig = lax.dot_general(cots, w, (((1,), (1,)), ((), ())), preferred_element_type=F32)
        ig = (ig * factor).astype(BF16)
        own[:, cols] = ig[:TOK]
        to_return[:, cols] = ig[TOK:]
    ahead[...] = total[:TOK] * factor
    to_return[:, YS * ROWS :] = (total[TOK:] * factor).astype(BF16)


def join_kernel(place, own, ahead, returned, projected, input_grad):
    zl = place[1]
    for f in range(YS):
        cols = slice(f * ROWS, (f + 1) * ROWS)
        input_grad[:, lanes(2 * f + zl)] = own[:, cols]
        input_grad[:, lanes(2 * f + 1 - zl)] = returned[:, cols]
    projected[...] = (ahead[...] + returned[:, YS * ROWS :].astype(F32)).astype(BF16)


def grad_kernel(factor, place, slab, both, keep, send):
    for out, col in ((send, 1 - place[1]), (keep, place[1])):
        total = None
        for f in range(0, YS, 2):
            x = slab[f : f + 2, :, lanes(col)].reshape(2 * TOK, ROWS)
            c = jnp.concatenate([both[f, ROWS:], both[f + 1, ROWS:]], 0)
            part = lax.dot_general(x, c, (((0,), (0,)), ((), ())), preferred_element_type=F32)
            total = part if f == 0 else total + part
        out[...] = (total * factor).astype(out.dtype)


def step_kernel(place, keep, sent, weight, moment, second, outer, momentum, half_sum, half_got, new_weight, new_moment, new_second):
    grad = keep[...] + sent[...].astype(F32)
    local = weight[...]
    outer_wide = outer[...].astype(F32)
    a, b = half_sum[...].astype(F32), half_got[...].astype(F32)
    low = place[2] == 0
    mean = jnp.concatenate([jnp.where(low, a, b), jnp.where(low, b, a)], 0) * (1.0 / REPLICAS)
    average = outer_wide - mean
    velocity = 0.9 * momentum[...].astype(F32) + average
    outer_new = outer_wide - 0.7 * (average + 0.9 * velocity)
    first_new = 0.8 * moment[...].astype(F32) + 0.2 * grad
    second_new = 0.95 * second[...].astype(F32) + 0.05 * grad * grad
    inner = local - 0.05 * (first_new / (jnp.sqrt(second_new) + 1e-08) + 0.1 * local)
    new_weight[...] = 0.5 * inner + 0.5 * outer_new
    new_moment[...] = first_new.astype(BF16)
    new_second[...] = second_new.astype(BF16)


def ring_shift(size, k):
    return [(i, (i + k) % size) for i in range(size)]


def add_pair(part):
    return (part[0].astype(F32) + part[1].astype(F32)).astype(BF16)


def ring_step(total, axis, k):
    return add_pair((total, lax.ppermute(total, axis, ring_shift(4, k))))


def core_sum(packed):
    core = lax.axis_index("core")
    n = ROWS // 2
    mine = lax.dynamic_slice_in_dim(packed, core * n, n)
    return add_pair((mine, lax.ppermute(lax.dynamic_slice_in_dim(packed, (1 - core) * n, n), "core", PAIR)))


def body(tokens, cotangent, weight, moment, second, outer_params, momentum):
    factor = 1.0 / math.sqrt(tokens.shape[1])
    place = jnp.stack([lax.axis_index("y"), lax.axis_index("zl"), lax.axis_index("core")]).astype(jnp.int32)
    sds = jax.ShapeDtypeStruct
    half = YS * ROWS
    flops = 2 * 2 * TOK * half * KV

    def run(kernel, args, outs, cost=0):
        return call(kernel, place, args, [whole(a.shape) for a in args], outs, cost)

    (packed,) = call(
        pack_kernel, None, [weight[0], cotangent],
        [pl.BlockSpec((ROWS, KV), lambda i: (0, 0)), pl.BlockSpec((TOK, KV), lambda i: (0, 0))],
        [sds((ROWS + TOK, KV), BF16)], 0,
    )
    both = lax.all_gather(packed, "y", axis=0, tiled=False)
    blocks, other = run(
        split_kernel, [tokens, cotangent], [sds((YS, TOK, 2 * ROWS), BF16), sds((TOK, half + KV), BF16)]
    )
    got = lax.ppermute(other, "zl", PAIR)

    packed, other = lax.optimization_barrier((packed, other))
    half_sum, got = lax.optimization_barrier((core_sum(packed), got))
    half_sum = ring_step(half_sum, "x", 2)
    blocks, half_sum = lax.optimization_barrier((blocks, half_sum))
    slab = lax.all_to_all(blocks, "y", 0, 0, tiled=True)
    half_sum = ring_step(half_sum, "x", 1)
    half_sum = ring_step(ring_step(half_sum, "zh", 2), "zh", 1)
    slab, half_sum = lax.optimization_barrier((slab, half_sum))

    own, ahead, to_return = run(
        functools.partial(product_kernel, factor), [tokens, cotangent, got, both],
        [sds((TOK, half), BF16), sds((TOK, KV), F32), sds((TOK, half + KV), BF16)], 2 * flops,
    )
    returned = lax.ppermute(to_return, "zl", PAIR)
    keep, send = run(
        functools.partial(grad_kernel, factor), [slab, both], [sds((ROWS, KV), F32), sds((ROWS, KV), BF16)], flops
    )
    send, half_sum = lax.optimization_barrier((send, half_sum))
    sent = lax.ppermute(send, "zl", PAIR)
    half_got = lax.ppermute(half_sum, "core", PAIR)
    projected, input_grad = run(
        join_kernel, [own, ahead, returned], [sds((TOK, KV), BF16), sds(tokens.shape, BF16)]
    )
    sent, projected = lax.optimization_barrier((sent, projected))
    new_weight, new_moment, new_second = run(
        step_kernel, [keep, sent, weight[0], moment[0], second[0], outer_params, momentum, half_sum, half_got],
        [sds((ROWS, KV), F32), sds((ROWS, KV), BF16), sds((ROWS, KV), BF16)], 40 * ROWS * KV,
    )
    return projected, input_grad, new_weight[None], new_moment[None], new_second[None]


def solution(mesh):
    fine = Mesh(mesh.devices.reshape(SIZES), NAMES)
    tok = P(NAMES, None)
    par = P(REPLICA, FSDP, None)
    outer = P(FSDP, None)
    return jax.shard_map(
        body,
        mesh=fine,
        in_specs=(tok, tok, par, par, par, outer, outer),
        out_specs=(tok, tok, par, par, par),
        check_vma=False,
    )
```

```python
import functools
import math

import jax
import jax.numpy as jnp
from jax import lax
from jax.experimental import pallas as pl
from jax.experimental.pallas import tpu as pltpu
from jax.sharding import Mesh, PartitionSpec as P

SIZES = (4, 4, 2, 8, 2)
NAMES = ("zh", "x", "core", "y", "zl")
REPLICA = ("zh", "x", "core")
FSDP = ("y", "zl")
PAIR = [(0, 1), (1, 0)]
BF16 = jnp.bfloat16
F32 = jnp.float32
YS = 8
REPLICAS = 32
ROWS = 256
TOK = 128
KV = 512
MIB = 1 << 20


def whole(shape):
    return pl.BlockSpec(shape, lambda *_: (0,) * len(shape))


def call(kernel, place, args, in_specs, outs, flops, scratch=()):
    size = sum(math.prod(a.shape) * a.dtype.itemsize for a in args)
    size += sum(math.prod(o.shape) * o.dtype.itemsize for o in outs)
    return pl.pallas_call(
        kernel,
        out_shape=outs,
        grid_spec=pltpu.PrefetchScalarGridSpec(
            num_scalar_prefetch=0 if place is None else 1,
            grid=(1,),
            in_specs=in_specs,
            out_specs=[whole(o.shape) for o in outs],
            scratch_shapes=scratch,
        ),
        compiler_params=pltpu.CompilerParams(vmem_limit_bytes=62 * MIB),
        cost_estimate=pl.CostEstimate(flops=flops, bytes_accessed=size, transcendentals=0),
    )(*([] if place is None else [place]), *args)


def lanes(index):
    return pl.ds(pl.multiple_of(index * ROWS, ROWS), ROWS)


def pack_kernel(weight, cot, packed):
    packed[:ROWS] = weight[...].astype(BF16)
    packed[ROWS:] = cot[...]


def split_kernel(place, tok, cot, blocks, other):
    other[:, YS * ROWS :] = cot[...]
    for f in range(YS):
        blocks[f] = tok[:, 2 * f * ROWS : (2 * f + 2) * ROWS]
        other[:, f * ROWS : (f + 1) * ROWS] = tok[:, lanes(2 * f + 1 - place[1])]


def product_kernel(factor, place, tok, cot, got, both, own, ahead, to_return):
    cots = jnp.concatenate([cot[...], got[:, YS * ROWS :]], 0)
    total = None
    for f in range(YS):
        w = both[f, :ROWS]
        cols = slice(f * ROWS, (f + 1) * ROWS)
        x = jnp.concatenate([tok[:, lanes(2 * f + place[1])], got[:, cols]], 0)
        part = jnp.dot(x, w, preferred_element_type=F32)
        total = part if f == 0 else total + part
        ig = lax.dot_general(cots, w, (((1,), (1,)), ((), ())), preferred_element_type=F32)
        ig = (ig * factor).astype(BF16)
        own[:, cols] = ig[:TOK]
        to_return[:, cols] = ig[TOK:]
    ahead[...] = total[:TOK] * factor
    to_return[:, YS * ROWS :] = (total[TOK:] * factor).astype(BF16)


def join_kernel(place, own, ahead, returned, projected, input_grad):
    zl = place[1]
    for f in range(YS):
        cols = slice(f * ROWS, (f + 1) * ROWS)
        input_grad[:, lanes(2 * f + zl)] = own[:, cols]
        input_grad[:, lanes(2 * f + 1 - zl)] = returned[:, cols]
    projected[...] = (ahead[...] + returned[:, YS * ROWS :].astype(F32)).astype(BF16)


def grad_kernel(factor, place, slab, both, keep, send):
    for out, col in ((send, 1 - place[1]), (keep, place[1])):
        total = None
        for f in range(0, YS, 2):
            x = slab[f : f + 2, :, lanes(col)].reshape(2 * TOK, ROWS)
            c = jnp.concatenate([both[f, ROWS:], both[f + 1, ROWS:]], 0)
            part = lax.dot_general(x, c, (((0,), (0,)), ((), ())), preferred_element_type=F32)
            total = part if f == 0 else total + part
        out[...] = (total * factor).astype(out.dtype)


def step_kernel(place, keep, sent, weight, moment, second, outer, momentum, half_sum, half_got, new_weight, new_moment, new_second):
    grad = keep[...] + sent[...].astype(F32)
    local = weight[...]
    outer_wide = outer[...].astype(F32)
    a, b = half_sum[...].astype(F32), half_got[...].astype(F32)
    low = place[2] == 0
    mean = jnp.concatenate([jnp.where(low, a, b), jnp.where(low, b, a)], 0) * (1.0 / REPLICAS)
    average = outer_wide - mean
    velocity = 0.9 * momentum[...].astype(F32) + average
    outer_new = outer_wide - 0.7 * (average + 0.9 * velocity)
    first_new = 0.8 * moment[...].astype(F32) + 0.2 * grad
    second_new = 0.95 * second[...].astype(F32) + 0.05 * grad * grad
    inner = local - 0.05 * (first_new / (jnp.sqrt(second_new) + 1e-08) + 0.1 * local)
    new_weight[...] = 0.5 * inner + 0.5 * outer_new
    new_moment[...] = first_new.astype(BF16)
    new_second[...] = second_new.astype(BF16)


def ring_shift(size, k):
    return [(i, (i + k) % size) for i in range(size)]


def add_pair(part):
    return (part[0].astype(F32) + part[1].astype(F32)).astype(BF16)


def ring_step(total, axis, k):
    return add_pair((total, lax.ppermute(total, axis, ring_shift(4, k))))


def core_sum(packed):
    core = lax.axis_index("core")
    n = ROWS // 2
    mine = lax.dynamic_slice_in_dim(packed, core * n, n)
    return add_pair((mine, lax.ppermute(lax.dynamic_slice_in_dim(packed, (1 - core) * n, n), "core", PAIR)))


def body(tokens, cotangent, weight, moment, second, outer_params, momentum):
    factor = 1.0 / math.sqrt(tokens.shape[1])
    place = jnp.stack([lax.axis_index("y"), lax.axis_index("zl"), lax.axis_index("core")]).astype(jnp.int32)
    sds = jax.ShapeDtypeStruct
    half = YS * ROWS
    flops = 2 * 2 * TOK * half * KV

    def run(kernel, args, outs, cost=0):
        return call(kernel, place, args, [whole(a.shape) for a in args], outs, cost)

    (packed,) = call(
        pack_kernel, None, [weight[0], cotangent],
        [pl.BlockSpec((ROWS, KV), lambda i: (0, 0)), pl.BlockSpec((TOK, KV), lambda i: (0, 0))],
        [sds((ROWS + TOK, KV), BF16)], 0,
    )
    both = lax.all_gather(packed, "y", axis=0, tiled=False)
    blocks, other = run(
        split_kernel, [tokens, cotangent], [sds((YS, TOK, 2 * ROWS), BF16), sds((TOK, half + KV), BF16)]
    )
    got = lax.ppermute(other, "zl", PAIR)

    packed, other = lax.optimization_barrier((packed, other))
    slab = lax.all_to_all(blocks, "y", 0, 0, tiled=True)
    half_sum = ring_step(ring_step(core_sum(packed), "x", 2), "x", 1)
    half_sum = ring_step(half_sum, "zh", 2)
    half_sum, slab = lax.optimization_barrier((half_sum, slab))
    half_sum = ring_step(half_sum, "zh", 1)
    slab, half_sum = lax.optimization_barrier((slab, half_sum))

    own, ahead, to_return = run(
        functools.partial(product_kernel, factor), [tokens, cotangent, got, both],
        [sds((TOK, half), BF16), sds((TOK, KV), F32), sds((TOK, half + KV), BF16)], 2 * flops,
    )
    returned = lax.ppermute(to_return, "zl", PAIR)
    keep, send = run(
        functools.partial(grad_kernel, factor), [slab, both], [sds((ROWS, KV), F32), sds((ROWS, KV), BF16)], flops
    )
    send, half_sum = lax.optimization_barrier((send, half_sum))
    sent = lax.ppermute(send, "zl", PAIR)
    half_got = lax.ppermute(half_sum, "core", PAIR)
    projected, input_grad = run(
        join_kernel, [own, ahead, returned], [sds((TOK, KV), BF16), sds(tokens.shape, BF16)]
    )
    sent, projected = lax.optimization_barrier((sent, projected))
    new_weight, new_moment, new_second = run(
        step_kernel, [keep, sent, weight[0], moment[0], second[0], outer_params, momentum, half_sum, half_got],
        [sds((ROWS, KV), F32), sds((ROWS, KV), BF16), sds((ROWS, KV), BF16)], 40 * ROWS * KV,
    )
    return projected, input_grad, new_weight[None], new_moment[None], new_second[None]


def solution(mesh):
    fine = Mesh(mesh.devices.reshape(SIZES), NAMES)
    tok = P(NAMES, None)
    par = P(REPLICA, FSDP, None)
    outer = P(FSDP, None)
    return jax.shard_map(
        body,
        mesh=fine,
        in_specs=(tok, tok, par, par, par, outer, outer),
        out_specs=(tok, tok, par, par, par),
        check_vma=False,
    )
```

```python
import functools
import math

import jax
import jax.numpy as jnp
from jax import lax
from jax.experimental import pallas as pl
from jax.experimental.pallas import tpu as pltpu
from jax.sharding import Mesh, PartitionSpec as P

SIZES = (4, 4, 2, 8, 2)
NAMES = ("zh", "x", "core", "y", "zl")
REPLICA = ("zh", "x", "core")
FSDP = ("y", "zl")
PAIR = [(0, 1), (1, 0)]
BF16 = jnp.bfloat16
F32 = jnp.float32
YS = 8
REPLICAS = 32
ROWS = 256
TOK = 128
KV = 512
MIB = 1 << 20


def whole(shape):
    return pl.BlockSpec(shape, lambda *_: (0,) * len(shape))


def call(kernel, place, args, in_specs, outs, flops, scratch=()):
    size = sum(math.prod(a.shape) * a.dtype.itemsize for a in args)
    size += sum(math.prod(o.shape) * o.dtype.itemsize for o in outs)
    return pl.pallas_call(
        kernel,
        out_shape=outs,
        grid_spec=pltpu.PrefetchScalarGridSpec(
            num_scalar_prefetch=0 if place is None else 1,
            grid=(1,),
            in_specs=in_specs,
            out_specs=[whole(o.shape) for o in outs],
            scratch_shapes=scratch,
        ),
        compiler_params=pltpu.CompilerParams(vmem_limit_bytes=62 * MIB),
        cost_estimate=pl.CostEstimate(flops=flops, bytes_accessed=size, transcendentals=0),
    )(*([] if place is None else [place]), *args)


def cut(array, shape, indices):
    return [(array, pl.BlockSpec(shape, functools.partial(lambda index, *_: index, index))) for index in indices]


def lanes(index):
    return pl.ds(pl.multiple_of(index * ROWS, ROWS), ROWS)


def pack_kernel(weight, cot, packed):
    packed[:ROWS] = weight[...].astype(BF16)
    packed[ROWS:] = cot[...]


def split_kernel(place, cot, *refs):
    tok, (blocks, other) = refs[:4], refs[4:]
    other[:, YS * ROWS :] = cot[...]
    for f in range(YS):
        i, j = divmod(f, 2)
        blocks[f] = tok[i][:, 2 * j * ROWS : (2 * j + 2) * ROWS]
        other[:, f * ROWS : (f + 1) * ROWS] = tok[i][:, lanes(2 * j + 1 - place[1])]


def product_kernel(factor, place, cot, *refs):
    tok, got, both, (own, ahead, to_return) = refs[:4], refs[4:9], refs[9:13], refs[13:]
    cots = jnp.concatenate([cot[...], got[4][...]], 0)
    total = None
    for f in range(YS):
        i, j = divmod(f, 2)
        w = both[i][j]
        cols = slice(f * ROWS, (f + 1) * ROWS)
        x = jnp.concatenate([tok[i][:, lanes(2 * j + place[1])], got[i][:, j * ROWS : (j + 1) * ROWS]], 0)
        part = jnp.dot(x, w, preferred_element_type=F32)
        total = part if f == 0 else total + part
        ig = lax.dot_general(cots, w, (((1,), (1,)), ((), ())), preferred_element_type=F32)
        ig = (ig * factor).astype(BF16)
        own[:, cols] = ig[:TOK]
        to_return[:, cols] = ig[TOK:]
    ahead[...] = total[:TOK] * factor
    to_return[:, YS * ROWS :] = (total[TOK:] * factor).astype(BF16)


def join_kernel(place, own, ahead, returned, projected, input_grad):
    zl = place[1]
    for f in range(YS):
        cols = slice(f * ROWS, (f + 1) * ROWS)
        input_grad[:, lanes(2 * f + zl)] = own[:, cols]
        input_grad[:, lanes(2 * f + 1 - zl)] = returned[:, cols]
    projected[...] = (ahead[...] + returned[:, YS * ROWS :].astype(F32)).astype(BF16)


def grad_kernel(factor, place, *refs):
    slab, cots, (keep, send) = refs[:4], refs[4:8], refs[8:]
    for out, col in ((send, 1 - place[1]), (keep, place[1])):
        total = None
        for i in range(4):
            x = slab[i][:, :, lanes(col)].reshape(2 * TOK, ROWS)
            c = cots[i][...].reshape(2 * TOK, KV)
            part = lax.dot_general(x, c, (((0,), (0,)), ((), ())), preferred_element_type=F32)
            total = part if i == 0 else total + part
        out[...] = (total * factor).astype(out.dtype)


def step_kernel(place, keep, sent, weight, moment, second, outer, momentum, half_sum, half_got, new_weight, new_moment, new_second):
    grad = keep[...] + sent[...].astype(F32)
    local = weight[...]
    outer_wide = outer[...].astype(F32)
    a, b = half_sum[...].astype(F32), half_got[...].astype(F32)
    low = place[2] == 0
    mean = jnp.concatenate([jnp.where(low, a, b), jnp.where(low, b, a)], 0) * (1.0 / REPLICAS)
    average = outer_wide - mean
    velocity = 0.9 * momentum[...].astype(F32) + average
    outer_new = outer_wide - 0.7 * (average + 0.9 * velocity)
    first_new = 0.8 * moment[...].astype(F32) + 0.2 * grad
    second_new = 0.95 * second[...].astype(F32) + 0.05 * grad * grad
    inner = local - 0.05 * (first_new / (jnp.sqrt(second_new) + 1e-08) + 0.1 * local)
    new_weight[...] = 0.5 * inner + 0.5 * outer_new
    new_moment[...] = first_new.astype(BF16)
    new_second[...] = second_new.astype(BF16)


def ring_shift(size, k):
    return [(i, (i + k) % size) for i in range(size)]


def add_pair(part):
    return (part[0].astype(F32) + part[1].astype(F32)).astype(BF16)


def ring_step(total, axis, k):
    return add_pair((total, lax.ppermute(total, axis, ring_shift(4, k))))


def core_sum(packed):
    core = lax.axis_index("core")
    n = ROWS // 2
    mine = lax.dynamic_slice_in_dim(packed, core * n, n)
    return add_pair((mine, lax.ppermute(lax.dynamic_slice_in_dim(packed, (1 - core) * n, n), "core", PAIR)))


def body(tokens, cotangent, weight, moment, second, outer_params, momentum):
    factor = 1.0 / math.sqrt(tokens.shape[1])
    place = jnp.stack([lax.axis_index("y"), lax.axis_index("zl"), lax.axis_index("core")]).astype(jnp.int32)
    sds = jax.ShapeDtypeStruct
    half = YS * ROWS
    flops = 2 * 2 * TOK * half * KV

    def run(kernel, args, outs, cost=0, cuts=()):
        specs = [whole(a.shape) for a in args] + [s for _, s in cuts]
        return call(kernel, place, args + [a for a, _ in cuts], specs, outs, cost)

    fours = range(4)
    token_cuts = cut(tokens, (TOK, 4 * ROWS), [(0, i) for i in fours])

    (packed,) = call(
        pack_kernel, None, [weight[0], cotangent],
        [pl.BlockSpec((ROWS, KV), lambda i: (0, 0)), pl.BlockSpec((TOK, KV), lambda i: (0, 0))],
        [sds((ROWS + TOK, KV), BF16)], 0,
    )
    both = lax.all_gather(packed, "y", axis=0, tiled=False)
    blocks, other = run(
        split_kernel, [cotangent], [sds((YS, TOK, 2 * ROWS), BF16), sds((TOK, half + KV), BF16)], 0, token_cuts
    )
    got = lax.ppermute(other, "zl", PAIR)

    packed, other = lax.optimization_barrier((packed, other))
    slab = lax.all_to_all(blocks, "y", 0, 0, tiled=True)
    half_sum = ring_step(ring_step(core_sum(packed), "x", 2), "x", 1)
    half_sum = ring_step(half_sum, "zh", 2)
    half_sum, slab = lax.optimization_barrier((half_sum, slab))
    half_sum = ring_step(half_sum, "zh", 1)
    slab, half_sum = lax.optimization_barrier((slab, half_sum))

    own, ahead, to_return = run(
        functools.partial(product_kernel, factor), [cotangent],
        [sds((TOK, half), BF16), sds((TOK, KV), F32), sds((TOK, half + KV), BF16)], 2 * flops,
        token_cuts + cut(got, (TOK, KV), [(0, i) for i in range(5)]) + cut(both, (2, ROWS, KV), [(i, 0, 0) for i in fours]),
    )
    returned = lax.ppermute(to_return, "zl", PAIR)
    keep, send = run(
        functools.partial(grad_kernel, factor), [], [sds((ROWS, KV), F32), sds((ROWS, KV), BF16)], flops,
        cut(slab, (2, TOK, 2 * ROWS), [(i, 0, 0) for i in fours]) + cut(both, (2, TOK, KV), [(i, 2, 0) for i in fours]),
    )
    send, half_sum = lax.optimization_barrier((send, half_sum))
    sent = lax.ppermute(send, "zl", PAIR)
    half_got = lax.ppermute(half_sum, "core", PAIR)
    projected, input_grad = run(
        join_kernel, [own, ahead, returned], [sds((TOK, KV), BF16), sds(tokens.shape, BF16)]
    )
    sent, projected = lax.optimization_barrier((sent, projected))
    new_weight, new_moment, new_second = run(
        step_kernel, [keep, sent, weight[0], moment[0], second[0], outer_params, momentum, half_sum, half_got],
        [sds((ROWS, KV), F32), sds((ROWS, KV), BF16), sds((ROWS, KV), BF16)], 40 * ROWS * KV,
    )
    return projected, input_grad, new_weight[None], new_moment[None], new_second[None]


def solution(mesh):
    fine = Mesh(mesh.devices.reshape(SIZES), NAMES)
    tok = P(NAMES, None)
    par = P(REPLICA, FSDP, None)
    outer = P(FSDP, None)
    return jax.shard_map(
        body,
        mesh=fine,
        in_specs=(tok, tok, par, par, par, outer, outer),
        out_specs=(tok, tok, par, par, par),
        check_vma=False,
    )
```

```python
import functools
import math

import jax
import jax.numpy as jnp
from jax import lax
from jax.experimental import pallas as pl
from jax.experimental.pallas import tpu as pltpu
from jax.sharding import Mesh, PartitionSpec as P

SIZES = (4, 4, 2, 8, 2)
NAMES = ("zh", "x", "core", "y", "zl")
REPLICA = ("zh", "x", "core")
FSDP = ("y", "zl")
PAIR = [(0, 1), (1, 0)]
BF16 = jnp.bfloat16
F32 = jnp.float32
YS = 8
REPLICAS = 32
ROWS = 256
TOK = 128
KV = 512
MIB = 1 << 20


def whole(shape):
    return pl.BlockSpec(shape, lambda *_: (0,) * len(shape))


def call(kernel, place, args, in_specs, outs, flops, scratch=()):
    size = sum(math.prod(a.shape) * a.dtype.itemsize for a in args)
    size += sum(math.prod(o.shape) * o.dtype.itemsize for o in outs)
    return pl.pallas_call(
        kernel,
        out_shape=outs,
        grid_spec=pltpu.PrefetchScalarGridSpec(
            num_scalar_prefetch=0 if place is None else 1,
            grid=(1,),
            in_specs=in_specs,
            out_specs=[whole(o.shape) for o in outs],
            scratch_shapes=scratch,
        ),
        compiler_params=pltpu.CompilerParams(vmem_limit_bytes=64 * MIB - (128 << 10)),
        cost_estimate=pl.CostEstimate(flops=flops, bytes_accessed=size, transcendentals=0),
    )(*([] if place is None else [place]), *args)


def cut(array, shape, indices):
    return [(array, pl.BlockSpec(shape, functools.partial(lambda index, *_: index, index))) for index in indices]


def lanes(index):
    return pl.ds(pl.multiple_of(index * ROWS, ROWS), ROWS)


def pack_kernel(weight, cot, packed):
    packed[:ROWS] = weight[...].astype(BF16)
    packed[ROWS:] = cot[...]


def split_kernel(*refs):
    tok, blocks = refs[:4], refs[4]
    for f in range(YS):
        i, j = divmod(f, 2)
        blocks[f] = tok[i][:, 2 * j * ROWS : (2 * j + 2) * ROWS]


def other_kernel(place, cot, *refs):
    tok, other = refs[:4], refs[4]
    other[:, YS * ROWS :] = cot[...]
    for f in range(YS):
        i, j = divmod(f, 2)
        other[:, f * ROWS : (f + 1) * ROWS] = tok[i][:, lanes(2 * j + 1 - place[1])]


def product_kernel(factor, place, cot, *refs):
    tok, got, both, (own, ahead, to_return) = refs[:4], refs[4:9], refs[9:13], refs[13:]
    cots = jnp.concatenate([cot[...], got[4][...]], 0)
    total = None
    for f in range(YS):
        i, j = divmod(f, 2)
        w = both[i][j]
        cols = slice(f * ROWS, (f + 1) * ROWS)
        x = jnp.concatenate([tok[i][:, lanes(2 * j + place[1])], got[i][:, j * ROWS : (j + 1) * ROWS]], 0)
        part = jnp.dot(x, w, preferred_element_type=F32)
        total = part if f == 0 else total + part
        ig = lax.dot_general(cots, w, (((1,), (1,)), ((), ())), preferred_element_type=F32)
        ig = (ig * factor).astype(BF16)
        own[:, cols] = ig[:TOK]
        to_return[:, cols] = ig[TOK:]
    ahead[...] = total[:TOK] * factor
    to_return[:, YS * ROWS :] = (total[TOK:] * factor).astype(BF16)


def join_kernel(place, own, ahead, returned, projected, input_grad):
    zl = place[1]
    for f in range(YS):
        cols = slice(f * ROWS, (f + 1) * ROWS)
        input_grad[:, lanes(2 * f + zl)] = own[:, cols]
        input_grad[:, lanes(2 * f + 1 - zl)] = returned[:, cols]
    projected[...] = (ahead[...] + returned[:, YS * ROWS :].astype(F32)).astype(BF16)


def grad_kernel(factor, place, *refs):
    slab, cots, (keep, send) = refs[:4], refs[4:8], refs[8:]
    for out, col in ((send, 1 - place[1]), (keep, place[1])):
        total = None
        for i in range(4):
            x = slab[i][:, :, lanes(col)].reshape(2 * TOK, ROWS)
            c = cots[i][...].reshape(2 * TOK, KV)
            part = lax.dot_general(x, c, (((0,), (0,)), ((), ())), preferred_element_type=F32)
            total = part if i == 0 else total + part
        out[...] = (total * factor).astype(out.dtype)


def step_kernel(place, keep, sent, weight, moment, second, outer, momentum, half_sum, half_got, new_weight, new_moment, new_second):
    grad = keep[...] + sent[...].astype(F32)
    local = weight[...]
    outer_wide = outer[...].astype(F32)
    a, b = half_sum[...].astype(F32), half_got[...].astype(F32)
    low = place[2] == 0
    mean = jnp.concatenate([jnp.where(low, a, b), jnp.where(low, b, a)], 0) * (1.0 / REPLICAS)
    average = outer_wide - mean
    velocity = 0.9 * momentum[...].astype(F32) + average
    outer_new = outer_wide - 0.7 * (average + 0.9 * velocity)
    first_new = 0.8 * moment[...].astype(F32) + 0.2 * grad
    second_new = 0.95 * second[...].astype(F32) + 0.05 * grad * grad
    inner = local - 0.05 * (first_new / (jnp.sqrt(second_new) + 1e-08) + 0.1 * local)
    new_weight[...] = 0.5 * inner + 0.5 * outer_new
    new_moment[...] = first_new.astype(BF16)
    new_second[...] = second_new.astype(BF16)


def ring_shift(size, k):
    return [(i, (i + k) % size) for i in range(size)]


def add_pair(part):
    return (part[0].astype(F32) + part[1].astype(F32)).astype(BF16)


def ring_step(total, axis, k):
    return add_pair((total, lax.ppermute(total, axis, ring_shift(4, k))))


def core_sum(packed):
    core = lax.axis_index("core")
    n = ROWS // 2
    mine = lax.dynamic_slice_in_dim(packed, core * n, n)
    return add_pair((mine, lax.ppermute(lax.dynamic_slice_in_dim(packed, (1 - core) * n, n), "core", PAIR)))


def body(tokens, cotangent, weight, moment, second, outer_params, momentum):
    factor = 1.0 / math.sqrt(tokens.shape[1])
    place = jnp.stack([lax.axis_index("y"), lax.axis_index("zl"), lax.axis_index("core")]).astype(jnp.int32)
    sds = jax.ShapeDtypeStruct
    half = YS * ROWS
    flops = 2 * 2 * TOK * half * KV

    def run(kernel, args, outs, cost=0, cuts=()):
        specs = [whole(a.shape) for a in args] + [s for _, s in cuts]
        return call(kernel, place, args + [a for a, _ in cuts], specs, outs, cost)

    fours = range(4)
    token_cuts = cut(tokens, (TOK, 4 * ROWS), [(0, i) for i in fours])

    (packed,) = call(
        pack_kernel, None, [weight[0], cotangent],
        [pl.BlockSpec((ROWS, KV), lambda i: (0, 0)), pl.BlockSpec((TOK, KV), lambda i: (0, 0))],
        [sds((ROWS + TOK, KV), BF16)], 0,
    )
    both = lax.all_gather(packed, "y", axis=0, tiled=False)
    (blocks,) = call(
        split_kernel, None, [tokens] * 4, [s for _, s in token_cuts], [sds((YS, TOK, 2 * ROWS), BF16)], 0
    )
    (other,) = run(other_kernel, [cotangent], [sds((TOK, half + KV), BF16)], 0, token_cuts)
    got = lax.ppermute(other, "zl", PAIR)

    packed, other = lax.optimization_barrier((packed, other))
    slab = lax.all_to_all(blocks, "y", 0, 0, tiled=True)
    half_sum = ring_step(ring_step(core_sum(packed), "x", 2), "x", 1)
    half_sum = ring_step(half_sum, "zh", 2)
    half_sum, slab = lax.optimization_barrier((half_sum, slab))
    half_sum = ring_step(half_sum, "zh", 1)
    slab, half_sum = lax.optimization_barrier((slab, half_sum))

    own, ahead, to_return = run(
        functools.partial(product_kernel, factor), [cotangent],
        [sds((TOK, half), BF16), sds((TOK, KV), F32), sds((TOK, half + KV), BF16)], 2 * flops,
        token_cuts + cut(got, (TOK, KV), [(0, i) for i in range(5)]) + cut(both, (2, ROWS, KV), [(i, 0, 0) for i in fours]),
    )
    returned = lax.ppermute(to_return, "zl", PAIR)
    keep, send = run(
        functools.partial(grad_kernel, factor), [], [sds((ROWS, KV), F32), sds((ROWS, KV), BF16)], flops,
        cut(slab, (2, TOK, 2 * ROWS), [(i, 0, 0) for i in fours]) + cut(both, (2, TOK, KV), [(i, 2, 0) for i in fours]),
    )
    send, half_sum = lax.optimization_barrier((send, half_sum))
    sent = lax.ppermute(send, "zl", PAIR)
    half_got = lax.ppermute(half_sum, "core", PAIR)
    projected, input_grad = run(
        join_kernel, [own, ahead, returned], [sds((TOK, KV), BF16), sds(tokens.shape, BF16)]
    )
    sent, projected = lax.optimization_barrier((sent, projected))
    new_weight, new_moment, new_second = run(
        step_kernel, [keep, sent, weight[0], moment[0], second[0], outer_params, momentum, half_sum, half_got],
        [sds((ROWS, KV), F32), sds((ROWS, KV), BF16), sds((ROWS, KV), BF16)], 40 * ROWS * KV,
    )
    return projected, input_grad, new_weight[None], new_moment[None], new_second[None]


def solution(mesh):
    fine = Mesh(mesh.devices.reshape(SIZES), NAMES)
    tok = P(NAMES, None)
    par = P(REPLICA, FSDP, None)
    outer = P(FSDP, None)
    return jax.shard_map(
        body,
        mesh=fine,
        in_specs=(tok, tok, par, par, par, outer, outer),
        out_specs=(tok, tok, par, par, par),
        check_vma=False,
    )
```

```python
import functools
import math

import jax
import jax.numpy as jnp
from jax import lax
from jax.experimental import pallas as pl
from jax.experimental.pallas import tpu as pltpu
from jax.sharding import Mesh, PartitionSpec as P

SIZES = (4, 4, 2, 8, 2)
NAMES = ("zh", "x", "core", "y", "zl")
REPLICA = ("zh", "x", "core")
FSDP = ("y", "zl")
PAIR = [(0, 1), (1, 0)]
BF16 = jnp.bfloat16
F32 = jnp.float32
YS = 8
REPLICAS = 32
ROWS = 256
TOK = 128
KV = 512
MIB = 1 << 20


def whole(shape):
    return pl.BlockSpec(shape, lambda *_: (0,) * len(shape))


def call(kernel, place, args, in_specs, outs, flops, scratch=()):
    size = sum(math.prod(a.shape) * a.dtype.itemsize for a in args)
    size += sum(math.prod(o.shape) * o.dtype.itemsize for o in outs)
    return pl.pallas_call(
        kernel,
        out_shape=outs,
        grid_spec=pltpu.PrefetchScalarGridSpec(
            num_scalar_prefetch=0 if place is None else 1,
            grid=(1,),
            in_specs=in_specs,
            out_specs=[whole(o.shape) for o in outs],
            scratch_shapes=scratch,
        ),
        compiler_params=pltpu.CompilerParams(vmem_limit_bytes=64 * MIB - (128 << 10)),
        cost_estimate=pl.CostEstimate(flops=flops, bytes_accessed=size, transcendentals=0),
    )(*([] if place is None else [place]), *args)


def cut(array, shape, indices):
    return [(array, pl.BlockSpec(shape, functools.partial(lambda index, *_: index, index))) for index in indices]


def lanes(index):
    return pl.ds(pl.multiple_of(index * ROWS, ROWS), ROWS)


def pack_kernel(weight, cot, packed):
    packed[:ROWS] = weight[...].astype(BF16)
    packed[ROWS:] = cot[...]


def split_kernel(*refs):
    tok, blocks = refs[:4], refs[4]
    for f in range(YS):
        i, j = divmod(f, 2)
        blocks[f] = tok[i][:, 2 * j * ROWS : (2 * j + 2) * ROWS]


def other_kernel(place, cot, *refs):
    tok, other = refs[:4], refs[4]
    other[:, YS * ROWS :] = cot[...]
    for f in range(YS):
        i, j = divmod(f, 2)
        other[:, f * ROWS : (f + 1) * ROWS] = tok[i][:, lanes(2 * j + 1 - place[1])]


def product_kernel(factor, place, cot, *refs):
    tok, got, both, (own, ahead, to_return) = refs[:4], refs[4:9], refs[9:13], refs[13:]
    cots = jnp.concatenate([cot[...], got[4][...]], 0)
    total = None
    for f in range(YS):
        i, j = divmod(f, 2)
        w = both[i][j]
        cols = slice(f * ROWS, (f + 1) * ROWS)
        x = jnp.concatenate([tok[i][:, lanes(2 * j + place[1])], got[i][:, j * ROWS : (j + 1) * ROWS]], 0)
        part = jnp.dot(x, w, preferred_element_type=F32)
        total = part if f == 0 else total + part
        ig = lax.dot_general(cots, w, (((1,), (1,)), ((), ())), preferred_element_type=F32)
        ig = (ig * factor).astype(BF16)
        own[:, cols] = ig[:TOK]
        to_return[:, cols] = ig[TOK:]
    ahead[...] = total[:TOK] * factor
    to_return[:, YS * ROWS :] = (total[TOK:] * factor).astype(BF16)


def join_kernel(place, own, ahead, returned, projected, input_grad):
    zl = place[1]
    for f in range(YS):
        cols = slice(f * ROWS, (f + 1) * ROWS)
        input_grad[:, lanes(2 * f + zl)] = own[:, cols]
        input_grad[:, lanes(2 * f + 1 - zl)] = returned[:, cols]
    projected[...] = (ahead[...] + returned[:, YS * ROWS :].astype(F32)).astype(BF16)


def grad_kernel(factor, place, *refs):
    slab, cots, (keep, send) = refs[:4], refs[4:8], refs[8:]
    for out, col in ((send, 1 - place[1]), (keep, place[1])):
        total = None
        for i in range(4):
            x = slab[i][:, :, lanes(col)].reshape(2 * TOK, ROWS)
            c = cots[i][...].reshape(2 * TOK, KV)
            part = lax.dot_general(x, c, (((0,), (0,)), ((), ())), preferred_element_type=F32)
            total = part if i == 0 else total + part
        out[...] = (total * factor).astype(out.dtype)


def step_kernel(place, keep, sent, weight, moment, second, outer, momentum, half_sum, half_got, new_weight, new_moment, new_second):
    grad = keep[...] + sent[...].astype(F32)
    local = weight[...]
    outer_wide = outer[...].astype(F32)
    a, b = half_sum[...].astype(F32), half_got[...].astype(F32)
    low = place[2] == 0
    mean = jnp.concatenate([jnp.where(low, a, b), jnp.where(low, b, a)], 0) * (1.0 / REPLICAS)
    average = outer_wide - mean
    velocity = 0.9 * momentum[...].astype(F32) + average
    outer_new = outer_wide - 0.7 * (average + 0.9 * velocity)
    first_new = 0.8 * moment[...].astype(F32) + 0.2 * grad
    second_new = 0.95 * second[...].astype(F32) + 0.05 * grad * grad
    inner = local - 0.05 * (first_new / (jnp.sqrt(second_new) + 1e-08) + 0.1 * local)
    new_weight[...] = 0.5 * inner + 0.5 * outer_new
    new_moment[...] = first_new.astype(BF16)
    new_second[...] = second_new.astype(BF16)


def ring_shift(size, k):
    return [(i, (i + k) % size) for i in range(size)]


def add_pair(part):
    return (part[0].astype(F32) + part[1].astype(F32)).astype(BF16)


def ring_step(total, axis, k):
    return add_pair((total, lax.ppermute(total, axis, ring_shift(4, k))))


def core_sum(packed):
    core = lax.axis_index("core")
    n = ROWS // 2
    mine = lax.dynamic_slice_in_dim(packed, core * n, n)
    return add_pair((mine, lax.ppermute(lax.dynamic_slice_in_dim(packed, (1 - core) * n, n), "core", PAIR)))


def body(tokens, cotangent, weight, moment, second, outer_params, momentum):
    factor = 1.0 / math.sqrt(tokens.shape[1])
    place = jnp.stack([lax.axis_index("y"), lax.axis_index("zl"), lax.axis_index("core")]).astype(jnp.int32)
    sds = jax.ShapeDtypeStruct
    half = YS * ROWS
    flops = 2 * 2 * TOK * half * KV

    def run(kernel, args, outs, cost=0, cuts=()):
        specs = [whole(a.shape) for a in args] + [s for _, s in cuts]
        return call(kernel, place, args + [a for a, _ in cuts], specs, outs, cost)

    fours = range(4)
    token_cuts = cut(tokens, (TOK, 4 * ROWS), [(0, i) for i in fours])

    (packed,) = call(
        pack_kernel, None, [weight[0], cotangent],
        [pl.BlockSpec((ROWS, KV), lambda i: (0, 0)), pl.BlockSpec((TOK, KV), lambda i: (0, 0))],
        [sds((ROWS + TOK, KV), BF16)], 0,
    )
    both = lax.all_gather(packed, "y", axis=0, tiled=False)
    (blocks,) = call(
        split_kernel, None, [tokens] * 4, [s for _, s in token_cuts], [sds((YS, TOK, 2 * ROWS), BF16)], 0
    )
    (other,) = run(other_kernel, [cotangent], [sds((TOK, half + KV), BF16)], 0, token_cuts)
    got = lax.ppermute(other, "zl", PAIR)

    packed, other = lax.optimization_barrier((packed, other))
    slab = lax.all_to_all(blocks, "y", 0, 0, tiled=True)
    half_sum = ring_step(ring_step(core_sum(packed), "x", 2), "x", 1)
    half_sum = ring_step(half_sum, "zh", 2)
    half_sum, slab = lax.optimization_barrier((half_sum, slab))
    came = lax.ppermute(half_sum, "zh", ring_shift(4, 1))
    slab, came = lax.optimization_barrier((slab, came))

    own, ahead, to_return = run(
        functools.partial(product_kernel, factor), [cotangent],
        [sds((TOK, half), BF16), sds((TOK, KV), F32), sds((TOK, half + KV), BF16)], 2 * flops,
        token_cuts + cut(got, (TOK, KV), [(0, i) for i in range(5)]) + cut(both, (2, ROWS, KV), [(i, 0, 0) for i in fours]),
    )
    returned = lax.ppermute(to_return, "zl", PAIR)
    keep, send = run(
        functools.partial(grad_kernel, factor), [], [sds((ROWS, KV), F32), sds((ROWS, KV), BF16)], flops,
        cut(slab, (2, TOK, 2 * ROWS), [(i, 0, 0) for i in fours]) + cut(both, (2, TOK, KV), [(i, 2, 0) for i in fours]),
    )
    send, came = lax.optimization_barrier((send, came))
    sent = lax.ppermute(send, "zl", PAIR)
    half_sum = add_pair((half_sum, came))
    half_got = lax.ppermute(half_sum, "core", PAIR)
    projected, input_grad = run(
        join_kernel, [own, ahead, returned], [sds((TOK, KV), BF16), sds(tokens.shape, BF16)]
    )
    sent, projected = lax.optimization_barrier((sent, projected))
    new_weight, new_moment, new_second = run(
        step_kernel, [keep, sent, weight[0], moment[0], second[0], outer_params, momentum, half_sum, half_got],
        [sds((ROWS, KV), F32), sds((ROWS, KV), BF16), sds((ROWS, KV), BF16)], 40 * ROWS * KV,
    )
    return projected, input_grad, new_weight[None], new_moment[None], new_second[None]


def solution(mesh):
    fine = Mesh(mesh.devices.reshape(SIZES), NAMES)
    tok = P(NAMES, None)
    par = P(REPLICA, FSDP, None)
    outer = P(FSDP, None)
    return jax.shard_map(
        body,
        mesh=fine,
        in_specs=(tok, tok, par, par, par, outer, outer),
        out_specs=(tok, tok, par, par, par),
        check_vma=False,
    )
```

```python
import functools
import math

import jax
import jax.numpy as jnp
from jax import lax
from jax.experimental import pallas as pl
from jax.experimental.pallas import tpu as pltpu
from jax.sharding import Mesh, PartitionSpec as P

SIZES = (4, 4, 2, 8, 2)
NAMES = ("zh", "x", "core", "y", "zl")
REPLICA = ("zh", "x", "core")
FSDP = ("y", "zl")
PAIR = [(0, 1), (1, 0)]
BF16 = jnp.bfloat16
F32 = jnp.float32
YS = 8
REPLICAS = 32
ROWS = 256
TOK = 128
KV = 512
MIB = 1 << 20


def whole(shape):
    return pl.BlockSpec(shape, lambda *_: (0,) * len(shape))


def call(kernel, place, args, in_specs, outs, flops, scratch=()):
    size = sum(math.prod(a.shape) * a.dtype.itemsize for a in args)
    size += sum(math.prod(o.shape) * o.dtype.itemsize for o in outs)
    grant = 64 * MIB - (128 << 10) if kernel in (join_kernel, step_kernel) else 62 * MIB
    return pl.pallas_call(
        kernel,
        out_shape=outs,
        grid_spec=pltpu.PrefetchScalarGridSpec(
            num_scalar_prefetch=0 if place is None else 1,
            grid=(1,),
            in_specs=in_specs,
            out_specs=[whole(o.shape) for o in outs],
            scratch_shapes=scratch,
        ),
        compiler_params=pltpu.CompilerParams(vmem_limit_bytes=grant),
        cost_estimate=pl.CostEstimate(flops=flops, bytes_accessed=size, transcendentals=0),
    )(*([] if place is None else [place]), *args)


def cut(array, shape, indices):
    return [(array, pl.BlockSpec(shape, functools.partial(lambda index, *_: index, index))) for index in indices]


def lanes(index):
    return pl.ds(pl.multiple_of(index * ROWS, ROWS), ROWS)


def pack_kernel(weight, cot, packed):
    packed[:ROWS] = weight[...].astype(BF16)
    packed[ROWS:] = cot[...]


def split_kernel(*refs):
    tok, blocks = refs[:4], refs[4]
    for f in range(YS):
        i, j = divmod(f, 2)
        blocks[f] = tok[i][:, 2 * j * ROWS : (2 * j + 2) * ROWS]


def other_kernel(place, cot, *refs):
    tok, other = refs[:4], refs[4]
    other[:, YS * ROWS :] = cot[...]
    for f in range(YS):
        i, j = divmod(f, 2)
        other[:, f * ROWS : (f + 1) * ROWS] = tok[i][:, lanes(2 * j + 1 - place[1])]


def product_kernel(factor, place, cot, *refs):
    tok, got, both, (own, ahead, to_return) = refs[:4], refs[4:9], refs[9:13], refs[13:]
    cots = jnp.concatenate([cot[...], got[4][...]], 0)
    total = None
    for f in range(YS):
        i, j = divmod(f, 2)
        w = both[i][j]
        cols = slice(f * ROWS, (f + 1) * ROWS)
        x = jnp.concatenate([tok[i][:, lanes(2 * j + place[1])], got[i][:, j * ROWS : (j + 1) * ROWS]], 0)
        part = jnp.dot(x, w, preferred_element_type=F32)
        total = part if f == 0 else total + part
        ig = lax.dot_general(cots, w, (((1,), (1,)), ((), ())), preferred_element_type=F32)
        ig = (ig * factor).astype(BF16)
        own[:, cols] = ig[:TOK]
        to_return[:, cols] = ig[TOK:]
    ahead[...] = total[:TOK] * factor
    to_return[:, YS * ROWS :] = (total[TOK:] * factor).astype(BF16)


def join_kernel(place, own, ahead, returned, projected, input_grad):
    zl = place[1]
    for f in range(YS):
        cols = slice(f * ROWS, (f + 1) * ROWS)
        input_grad[:, lanes(2 * f + zl)] = own[:, cols]
        input_grad[:, lanes(2 * f + 1 - zl)] = returned[:, cols]
    projected[...] = (ahead[...] + returned[:, YS * ROWS :].astype(F32)).astype(BF16)


def grad_kernel(factor, place, *refs):
    slab, cots, (keep, send) = refs[:4], refs[4:8], refs[8:]
    for out, col in ((send, 1 - place[1]), (keep, place[1])):
        total = None
        for i in range(4):
            x = slab[i][:, :, lanes(col)].reshape(2 * TOK, ROWS)
            c = cots[i][...].reshape(2 * TOK, KV)
            part = lax.dot_general(x, c, (((0,), (0,)), ((), ())), preferred_element_type=F32)
            total = part if i == 0 else total + part
        out[...] = (total * factor).astype(out.dtype)


def step_kernel(place, keep, sent, weight, moment, second, outer, momentum, half_sum, half_got, new_weight, new_moment, new_second):
    grad = keep[...] + sent[...].astype(F32)
    local = weight[...]
    outer_wide = outer[...].astype(F32)
    a, b = half_sum[...].astype(F32), half_got[...].astype(F32)
    low = place[2] == 0
    mean = jnp.concatenate([jnp.where(low, a, b), jnp.where(low, b, a)], 0) * (1.0 / REPLICAS)
    average = outer_wide - mean
    velocity = 0.9 * momentum[...].astype(F32) + average
    outer_new = outer_wide - 0.7 * (average + 0.9 * velocity)
    first_new = 0.8 * moment[...].astype(F32) + 0.2 * grad
    second_new = 0.95 * second[...].astype(F32) + 0.05 * grad * grad
    inner = local - 0.05 * (first_new / (jnp.sqrt(second_new) + 1e-08) + 0.1 * local)
    new_weight[...] = 0.5 * inner + 0.5 * outer_new
    new_moment[...] = first_new.astype(BF16)
    new_second[...] = second_new.astype(BF16)


def ring_shift(size, k):
    return [(i, (i + k) % size) for i in range(size)]


def add_pair(part):
    return (part[0].astype(F32) + part[1].astype(F32)).astype(BF16)


def ring_step(total, axis, k):
    return add_pair((total, lax.ppermute(total, axis, ring_shift(4, k))))


def core_sum(packed):
    core = lax.axis_index("core")
    n = ROWS // 2
    mine = lax.dynamic_slice_in_dim(packed, core * n, n)
    return add_pair((mine, lax.ppermute(lax.dynamic_slice_in_dim(packed, (1 - core) * n, n), "core", PAIR)))


def body(tokens, cotangent, weight, moment, second, outer_params, momentum):
    factor = 1.0 / math.sqrt(tokens.shape[1])
    place = jnp.stack([lax.axis_index("y"), lax.axis_index("zl"), lax.axis_index("core")]).astype(jnp.int32)
    sds = jax.ShapeDtypeStruct
    half = YS * ROWS
    flops = 2 * 2 * TOK * half * KV

    def run(kernel, args, outs, cost=0, cuts=()):
        specs = [whole(a.shape) for a in args] + [s for _, s in cuts]
        return call(kernel, place, args + [a for a, _ in cuts], specs, outs, cost)

    fours = range(4)
    token_cuts = cut(tokens, (TOK, 4 * ROWS), [(0, i) for i in fours])

    (packed,) = call(
        pack_kernel, None, [weight[0], cotangent],
        [pl.BlockSpec((ROWS, KV), lambda i: (0, 0)), pl.BlockSpec((TOK, KV), lambda i: (0, 0))],
        [sds((ROWS + TOK, KV), BF16)], 0,
    )
    both = lax.all_gather(packed, "y", axis=0, tiled=False)
    (blocks,) = call(
        split_kernel, None, [tokens] * 4, [s for _, s in token_cuts], [sds((YS, TOK, 2 * ROWS), BF16)], 0
    )
    (other,) = run(other_kernel, [cotangent], [sds((TOK, half + KV), BF16)], 0, token_cuts)
    got = lax.ppermute(other, "zl", PAIR)

    packed, other = lax.optimization_barrier((packed, other))
    slab = lax.all_to_all(blocks, "y", 0, 0, tiled=True)
    half_sum = ring_step(ring_step(core_sum(packed), "x", 2), "x", 1)
    half_sum = ring_step(half_sum, "zh", 2)
    half_sum, slab = lax.optimization_barrier((half_sum, slab))
    half_sum = ring_step(half_sum, "zh", 1)
    slab, half_sum = lax.optimization_barrier((slab, half_sum))

    own, ahead, to_return = run(
        functools.partial(product_kernel, factor), [cotangent],
        [sds((TOK, half), BF16), sds((TOK, KV), F32), sds((TOK, half + KV), BF16)], 2 * flops,
        token_cuts + cut(got, (TOK, KV), [(0, i) for i in range(5)]) + cut(both, (2, ROWS, KV), [(i, 0, 0) for i in fours]),
    )
    returned = lax.ppermute(to_return, "zl", PAIR)
    keep, send = run(
        functools.partial(grad_kernel, factor), [], [sds((ROWS, KV), F32), sds((ROWS, KV), BF16)], flops,
        cut(slab, (2, TOK, 2 * ROWS), [(i, 0, 0) for i in fours]) + cut(both, (2, TOK, KV), [(i, 2, 0) for i in fours]),
    )
    send, half_sum = lax.optimization_barrier((send, half_sum))
    sent = lax.ppermute(send, "zl", PAIR)
    half_got = lax.ppermute(half_sum, "core", PAIR)
    projected, input_grad = run(
        join_kernel, [own, ahead, returned], [sds((TOK, KV), BF16), sds(tokens.shape, BF16)]
    )
    sent, projected = lax.optimization_barrier((sent, projected))
    new_weight, new_moment, new_second = run(
        step_kernel, [keep, sent, weight[0], moment[0], second[0], outer_params, momentum, half_sum, half_got],
        [sds((ROWS, KV), F32), sds((ROWS, KV), BF16), sds((ROWS, KV), BF16)], 40 * ROWS * KV,
    )
    return projected, input_grad, new_weight[None], new_moment[None], new_second[None]


def solution(mesh):
    fine = Mesh(mesh.devices.reshape(SIZES), NAMES)
    tok = P(NAMES, None)
    par = P(REPLICA, FSDP, None)
    outer = P(FSDP, None)
    return jax.shard_map(
        body,
        mesh=fine,
        in_specs=(tok, tok, par, par, par, outer, outer),
        out_specs=(tok, tok, par, par, par),
        check_vma=False,
    )
```
